32 devices in a mesh: wide: 8 (over z, core), tall: 4 (over y, x).
Axes of the slice: x: 2, y: 2, z: 4, core: 2. Of those that a mesh axis runs over, the one named last changes fastest.
Arguments:
- initial: float32 [16384, 16384], P(('wide', 'tall')), as said below
- child_tiles: float32 [1024, 128, 128], P(('wide', 'tall')), may hold values from -0.75 to 0.75
- child_targets: int32 [1024, 2], P(('wide', 'tall')), may hold values from 0 to 127, as said below
Outputs:
- front: float32 [16384, 16384], P('tall', 'wide')
The draws below stay inside these ranges and needn't reach their ends.
Inputs may be any that keep to these rules, and one draw needn't show every extreme that they name: initial is symmetric, and assembled with its lower triangle mirrored is positive definite. `child_targets`: tile t * 8 + k of a device (t < 4, k < 8) lands on a block whose rows lie in the 512 rows of initial held by device g * 4 + t, g being the sender's index along wide; such a block's grid owner is the device at tall index (block row * 128 // 512) mod 4 and wide index (block column * 128 // 512) mod 8; the 8 tiles of one device with the same t go to 8 different grid owners, so one device sends at most one tile to one owner; in every grid row some owner gets one tile from every device.
All inputs are finite; a program needn't handle non-finite values.
Results may differ from the reference program's by a relative error of at most 0.0003.
Values sent between devices are 32-bit elements; how exact they have to be, the bound alone decides.
No kernel may reach another device: no remote copies, remote signals or barrier semaphores. Data moves between devices by JAX's collectives and lax.ppermute only.
A program may use at most 256 MiB of HBM per device.

```python
import jax
import jax.numpy as jnp
from jax import lax

F = 16384
PANEL = 512
CH = 128
PANELS = 2
K = 8
CT = 32
ROWB = 512
N_WIDE = 8
N_TALL = 4
DEVICES = 32


def draw_initial(key, part):
    key_point, key_noise, key_diag = jax.random.split(jax.random.fold_in(key, 5), 3)
    points = jax.random.uniform(key_point, (3, F), jnp.float32, 0.0, 1.0)
    noise = jnp.clip(jax.random.normal(key_noise, (F, F), jnp.float32), -3.0, 3.0) * 0.25
    distance_sq = (points[0][:, None] - points[0][None, :]) ** 2
    distance_sq = distance_sq + (points[1][:, None] - points[1][None, :]) ** 2
    distance_sq = distance_sq + (points[2][:, None] - points[2][None, :]) ** 2
    kernel = jnp.exp(-jnp.sqrt(distance_sq) / 0.35)
    mirrored = (noise + noise.T) * 0.70710678
    root_order = jnp.sqrt(jnp.float32(F))
    lanes = jnp.arange(F, dtype=jnp.int32)
    diagonal = jax.random.uniform(key_diag, (F,), jnp.float32, 2.0, 4.0) * root_order
    matrix = 4.0 * root_order * kernel + jnp.where(lanes[:, None] == lanes[None, :], diagonal[:, None], mirrored)
    return matrix


def draw_child_targets(key, part):
    key_hot, key_score, key_row, key_tile, key_inner = jax.random.split(jax.random.fold_in(key, 11), 5)
    hot_wide = jax.random.randint(key_hot, (N_TALL,), 0, N_WIDE)
    hot_wide = hot_wide.at[N_TALL - 1].set(N_WIDE - 1)
    scores = jax.random.randint(key_score, (DEVICES, N_TALL, N_WIDE), 0, 65536)
    lanes = jnp.arange(N_WIDE, dtype=jnp.int32)
    scores = jnp.where(lanes[None, None, :] == hot_wide[None, :, None], 131072, scores)
    scores = scores * N_WIDE + lanes[None, None, :]
    best_scores, chosen = lax.top_k(scores, K)
    chosen = jnp.sort(chosen.astype(jnp.int32), axis=-1)
    devices = jnp.arange(DEVICES, dtype=jnp.int32)[:, None, None]
    talls = jnp.arange(N_TALL, dtype=jnp.int32)[None, :, None]
    owner_row = devices // N_TALL * N_TALL + talls
    row_blocks = ROWB // CH
    row_pick = jax.random.randint(key_row, (DEVICES, N_TALL, K), 0, row_blocks)
    row_pick = row_pick.at[DEVICES - 1, N_TALL - 1, K - 1].set(row_blocks - 1)
    row_pick = row_pick.at[0, 0, 0].set(0)
    block_row = owner_row * row_blocks + row_pick
    tile_at = jax.random.randint(key_tile, (DEVICES, N_TALL, K), 0, F // (PANEL * N_WIDE))
    tile_at = tile_at.at[DEVICES - 1, N_TALL - 1, K - 1].set(F // (PANEL * N_WIDE) - 1)
    inner_at = jax.random.randint(key_inner, (DEVICES, N_TALL, K), 0, PANEL // CH)
    inner_at = inner_at.at[DEVICES - 1, N_TALL - 1, K - 1].set(PANEL // CH - 1)
    block_col = (tile_at * N_WIDE + chosen) * (PANEL // CH) + inner_at
    return jnp.stack([block_row, block_col], axis=-1).reshape(DEVICES * CT, 2).astype(jnp.int32)


def steps_of(key, dims, pieces, smallest, top_value):
    loudness = 1.0
    for axis_at, parts in pieces:
        steps = jax.random.uniform(jax.random.fold_in(jax.random.fold_in(key, 6), axis_at), (parts,), jnp.float32, smallest / len(pieces), top_value / len(pieces))
        loudness = loudness * jnp.repeat(jnp.exp(steps), dims[axis_at] // parts).reshape((-1,) + (1,) * (len(dims) - 1 - axis_at))
    return loudness


def normal_values(own_key, dims, scale, limit, cuts=(), kind=jnp.bfloat16):
    level = steps_of(own_key, dims, cuts, -0.22, 0.18) if cuts else 1.0
    entries = jax.random.normal(own_key, dims, jnp.float32) * scale * level
    return jnp.minimum(jnp.maximum(entries, -limit), limit).astype(kind)


def setup_inputs(seed: int = 0) -> dict:
    keys = jax.random.split(jax.random.key(seed), 4)
    initial = draw_initial(jax.random.fold_in(keys[3], 71), 0)
    child_tiles = normal_values(keys[1], (DEVICES * CT, CH, CH), 0.25, 0.75, ((0, 32),), jnp.float32)
    child_targets = draw_child_targets(jax.random.fold_in(keys[3], 71), 0)
    return {"initial": initial, "child_tiles": child_tiles, "child_targets": child_targets}


full_precision = lax.Precision.HIGHEST

def reference(initial, child_tiles, child_targets):
    front_order = initial.shape[0]
    offsets = jnp.arange(CH, dtype=jnp.int32)
    row_index = (child_targets[:, 0] * CH)[:, None, None] + offsets[None, :, None]
    col_index = (child_targets[:, 1] * CH)[:, None, None] + offsets[None, None, :]
    matrix = initial.at[row_index, col_index].add(child_tiles)
    identity = jnp.eye(PANEL, dtype=jnp.float32)
    for panel_at in range(PANELS):
        low_row = panel_at * PANEL
        high_row = low_row + PANEL
        diag_block = matrix[low_row:high_row, low_row:high_row]
        factor = jnp.linalg.cholesky(jnp.tril(diag_block) + jnp.tril(diag_block, -1).T)
        inverse = lax.linalg.triangular_solve(factor, identity, left_side=True, lower=True)
        solved = jnp.dot(matrix[high_row:, low_row:high_row].astype(jnp.float32), inverse.T.astype(jnp.float32), precision=full_precision, preferred_element_type=jnp.float32)
        matrix = matrix.at[low_row:high_row, low_row:high_row].set(jnp.tril(factor) + jnp.triu(diag_block, 1))
        matrix = matrix.at[high_row:, low_row:high_row].set(solved)
        change = jnp.dot(solved.astype(jnp.float32), solved.T.astype(jnp.float32), precision=full_precision, preferred_element_type=jnp.float32)
        matrix = matrix.at[high_row:, high_row:].add(-change)
    tall_rows = front_order // N_TALL
    wide_cols = front_order // N_WIDE
    matrix = matrix.reshape(tall_rows // ROWB, N_TALL, ROWB, front_order).transpose(1, 0, 2, 3).reshape(front_order, front_order)
    matrix = matrix.reshape(front_order, wide_cols // PANEL, N_WIDE, PANEL).transpose(0, 2, 1, 3).reshape(front_order, front_order)
    return matrix
```

```python
import functools

import jax
import jax.numpy as jnp
import numpy as np
from jax import lax
from jax.experimental import pallas as pl
from jax.experimental.pallas import tpu as pltpu
from jax.sharding import PartitionSpec as P

PANEL = 512
PANELS = 2
BOTH = ("wide", "tall")
VMEM_LIMIT = 56 * 1024 * 1024
full_precision = lax.Precision.HIGHEST


def full_dot(left, right, dims=((1,), (0,))):
    return lax.dot_general(
        left, right, (dims, ((), ())), precision=full_precision, preferred_element_type=jnp.float32
    )


def iota(shape, axis):
    return lax.broadcasted_iota(jnp.int32, shape, axis)


def factor_block(work, edge):
    group = 8
    wide = 2 * edge
    lanes = iota((group, edge), 1)
    row = iota((group, 1), 0)

    def step(s, carry):
        low = pl.multiple_of(s * group, group)
        strip = work[pl.ds(low, group), :]
        left = strip[:, :edge]
        cols = [
            jnp.sum(jnp.where(lanes == low + i, left, 0.0), axis=1, keepdims=True)
            for i in range(group)
        ]
        for i in range(group):
            pivot = cols[i][i : i + 1]
            scale = lax.rsqrt(pivot)
            scale = scale * (1.5 - 0.5 * pivot * scale * scale)
            column = jnp.where(row > i, cols[i] * scale, 0.0)
            top = strip[i : i + 1] * scale
            strip = jnp.where(row == i, top, strip - column * top)
            for m in range(i + 1, group):
                cols[m] = cols[m] - column * column[m : m + 1]
        work[pl.ds(low, group), :] = strip
        left = jnp.where(lanes >= low + group, strip[:, :edge], 0.0)
        work[...] = work[...] - full_dot(left, strip, ((0,), (0,)))
        return carry

    lax.fori_loop(0, edge // group, step, 0)


def factor_kernel(diag, factors, inverses, below, square, work):
    edge = work.shape[0]
    wide = PANEL
    lower = iota((wide, wide), 0) >= iota((wide, wide), 1)
    small = iota((edge, edge), 0) >= iota((edge, edge), 1)
    eye = (iota((edge, edge), 0) == iota((edge, edge), 1)).astype(jnp.float32)
    steps = wide // edge
    for p in range(PANELS):
        own = pl.ds(p * wide, wide)
        block = diag[own, own]
        block = jnp.where(lower, block, block.T)
        for before in range(p):
            rows = below[pl.ds((p - 1) * wide, wide), pl.ds(before * wide, wide)]
            block = block - full_dot(rows, rows, ((1,), (1,)))
        square[...] = block
        factors[p] = jnp.zeros((wide, wide), jnp.float32)
        inverses[p] = jnp.zeros((wide, wide), jnp.float32)
        for b in range(steps):
            at = pl.ds(b * edge, edge)
            work[:, :edge] = square[at, at]
            work[:, edge:] = eye
            factor_block(work, edge)
            factors[p, at, at] = jnp.where(small, work[:, :edge].T, 0.0)
            inverse = jnp.where(small, work[:, edge:], 0.0)
            inverses[p, at, at] = inverse
            if b + 1 < steps:
                rest = pl.ds((b + 1) * edge, wide - (b + 1) * edge)
                under = full_dot(square[rest, at], inverse, ((1,), (1,)))
                factors[p, rest, at] = under
                square[rest, rest] = square[rest, rest] - full_dot(under, under, ((1,), (1,)))
            if b > 0:
                past = pl.ds(0, b * edge)
                inner = full_dot(factors[p, at, past], inverses[p, past, past])
                inverses[p, at, past] = -full_dot(inverse, inner)
        for after in range(p + 1, PANELS):
            there = pl.ds(after * wide, wide)
            rows = diag[there, own]
            for before in range(p):
                rows = rows - full_dot(
                    below[pl.ds((after - 1) * wide, wide), pl.ds(before * wide, wide)],
                    below[pl.ds((p - 1) * wide, wide), pl.ds(before * wide, wide)],
                    ((1,), (1,)),
                )
            below[pl.ds((after - 1) * wide, wide), own] = full_dot(rows, inverses[p], ((1,), (1,)))


def add_blocks(base, tiles, block_index, tile_edge):
    base_rows, base_cols = base.shape
    row_count = base_rows // tile_edge
    col_count = base_cols // tile_edge
    slot_ids = jnp.arange(row_count * col_count, dtype=jnp.int32)
    selector = (slot_ids[:, None] == block_index[None, :]).astype(jnp.float32)
    summed = full_dot(selector, tiles)
    summed = summed.reshape(row_count, col_count, tile_edge, tile_edge).transpose(0, 2, 1, 3)
    return base + summed.reshape(base_rows, base_cols)


def block_tables(wanted, tall_size):
    owners = wanted % tall_size
    slots_at = wanted // tall_size
    width_wanted = wanted.shape[1]
    same_owner = owners[:, :, None] == owners[:, None, :]
    earlier = np.tril(np.ones((width_wanted, width_wanted), dtype=np.int32), -1)[None, :, :] > 0
    ranks = np.sum(same_owner & earlier, axis=2)
    piece_depth = int(np.max(ranks)) + 1
    talls = np.arange(tall_size)
    places = np.arange(piece_depth)
    matches = (owners[:, None, None, :] == talls[None, :, None, None]) & (
        ranks[:, None, None, :] == places[None, None, :, None]
    )
    senders = np.sum(matches * slots_at[:, None, None, :], axis=3).astype(np.int32)
    receivers = (owners * piece_depth + ranks).astype(np.int32)
    return (senders, receivers)


def copy_kernel(table, source, target):
    target[0] = source[...]


def pack(slab, columns):
    rows = slab.shape[0]
    count = columns.shape[0]
    return pl.pallas_call(
        copy_kernel,
        grid_spec=pltpu.PrefetchScalarGridSpec(
            num_scalar_prefetch=1,
            grid=(count,),
            in_specs=[pl.BlockSpec((rows, PANEL), lambda n, table: (0, table[n]))],
            out_specs=pl.BlockSpec((1, rows, PANEL), lambda n, table: (n, 0, 0)),
        ),
        out_shape=jax.ShapeDtypeStruct((count, rows, PANEL), jnp.float32),
        cost_estimate=pl.CostEstimate(
            flops=0, bytes_accessed=2 * count * rows * PANEL * 4, transcendentals=0
        ),
        name="pack",
    )(columns.astype(jnp.int32), slab)


def factor_panels(diag):
    square = jax.ShapeDtypeStruct((PANELS, PANEL, PANEL), jnp.float32)
    rest = (PANELS - 1) * PANEL
    edge = 128
    return pl.pallas_call(
        factor_kernel,
        out_shape=(square, square, jax.ShapeDtypeStruct((rest, rest), jnp.float32)),
        scratch_shapes=[
            pltpu.VMEM((PANEL, PANEL), jnp.float32),
            pltpu.VMEM((edge, 2 * edge), jnp.float32),
        ],
        compiler_params=pltpu.CompilerParams(vmem_limit_bytes=VMEM_LIMIT),
        cost_estimate=pl.CostEstimate(
            flops=90_000_000_000, bytes_accessed=10_000_000, transcendentals=0
        ),
        name="factor",
    )(diag)


def split(value):
    high = value.astype(jnp.bfloat16)
    return high, (value - high.astype(jnp.float32)).astype(jnp.bfloat16)


def solve_kernel(turned, parts, table, *refs):
    raws = refs[:parts]
    inverses, below = refs[parts : parts + 2]
    outs, raw = refs[parts + 2 : -1], refs[-1]
    rows = raw.shape[0]
    for i, ref in enumerate(raws):

        @pl.when(table[1, 0] == i)
        def _(ref=ref):
            raw[...] = ref[0]

    at = table[0, pl.program_id(0)] + iota((rows, 1), 0)
    solved_0 = full_dot(raw[:, :PANEL], inverses[0], ((1,), (1,)))
    solved_0 = jnp.where(at >= PANEL, solved_0, 0.0)
    right = raw[:, PANEL:] - full_dot(solved_0, below[...], ((1,), (1,)))
    solved_1 = full_dot(right, inverses[1], ((1,), (1,)))
    solved_1 = jnp.where(at >= 2 * PANEL, solved_1, 0.0)
    for p, part in enumerate((solved_0, solved_1)):
        span = pl.ds(p * PANEL, PANEL)
        if turned:
            outs[0][0, span, :], outs[1][0, span, :] = split(part.T)
        else:
            outs[0][0, :, span] = part


def solve(raws, which, first_row, inverses, below, turned=False):
    count, rows, depth = raws[0].shape
    if turned:
        out_shape = [jax.ShapeDtypeStruct((count, depth, rows), jnp.bfloat16)] * 2
        out_specs = [pl.BlockSpec((1, depth, rows), lambda n, table: (n, 0, 0))] * 2
    else:
        out_shape = [jax.ShapeDtypeStruct((count, rows, depth), jnp.float32)]
        out_specs = [pl.BlockSpec((1, rows, depth), lambda n, table: (n, 0, 0))]

    def held(i):
        return pl.BlockSpec(
            (1, rows, depth), lambda n, table: (jnp.where(table[1, 0] == i, n, 0), 0, 0)
        )

    table = jnp.stack([first_row, jnp.full_like(first_row, 1) * which]).astype(jnp.int32)
    return pl.pallas_call(
        functools.partial(solve_kernel, turned, len(raws)),
        grid_spec=pltpu.PrefetchScalarGridSpec(
            num_scalar_prefetch=1,
            grid=(count,),
            in_specs=[held(i) for i in range(len(raws))]
            + [
                pl.BlockSpec(inverses.shape, lambda n, table: (0, 0, 0)),
                pl.BlockSpec(below.shape, lambda n, table: (0, 0)),
            ],
            out_specs=out_specs,
            scratch_shapes=[pltpu.VMEM((rows, depth), jnp.float32)],
        ),
        out_shape=out_shape,
        compiler_params=pltpu.CompilerParams(vmem_limit_bytes=VMEM_LIMIT),
        cost_estimate=pl.CostEstimate(
            flops=36 * count * rows * PANEL * PANEL,
            bytes_accessed=8 * count * rows * depth,
            transcendentals=0,
        ),
        name="solve",
    )(table, *raws, inverses, below)


def update_kernel(turned, row_parts, place, tile_place, *refs):
    pieces = refs[: len(turned)]
    row_refs = refs[len(turned) : len(turned) + row_parts]
    col_hi, col_lo, factors, tiles = refs[len(turned) + row_parts : len(turned) + row_parts + 4]
    out, row_hi, row_lo = refs[-3:]
    step = pl.program_id(0)
    rows, width = out.shape
    edge = tiles.shape[2]
    slot = place[3, step]
    at = place[4, step]
    first_row = place[5, step]
    panel = place[6, step]
    kind = place[7, step]
    fresh = (step == 0) | (slot != place[3, jnp.maximum(step - 1, 0)])
    for i, ref in enumerate(row_refs):

        @pl.when(fresh & (place[8, step] == i))
        def _(ref=ref):
            row_hi[...], row_lo[...] = split(ref[0])

    for i, ref in enumerate(pieces):

        @pl.when(kind == i)
        def _(i=i, ref=ref):
            out[...] = ref[0].T if turned[i] else ref[0]

    change = jnp.dot(row_hi[...], col_hi[at], preferred_element_type=jnp.float32)
    change += jnp.dot(row_hi[...], col_lo[at], preferred_element_type=jnp.float32)
    change += jnp.dot(row_lo[...], col_hi[at], preferred_element_type=jnp.float32)

    @pl.when(kind >= len(pieces))
    def _():
        out[...] = -change

    @pl.when(kind < len(pieces))
    def _():
        out[...] = out[...] - change

    def add_tile(n, carry):
        at_row = pl.multiple_of(tile_place[1, n] * edge, edge)
        at_col = pl.multiple_of(tile_place[2, n] * edge, edge)
        spot = (pl.ds(at_row, edge), pl.ds(at_col, edge))
        out[spot] = out[spot] + tiles[tile_place[0, n], :edge, :]
        return carry

    lax.fori_loop(place[2, step], place[9, step], add_tile, 0)
    for p in range(PANELS):
        for i, ref in enumerate(row_refs):

            @pl.when((panel == p) & (first_row >= width) & (place[8, step] == i))
            def _(p=p, ref=ref):
                out[...] = ref[0, :, p * PANEL : (p + 1) * PANEL]

        @pl.when((panel == p) & (first_row >= 0) & (first_row < width))
        def _(p=p):
            row = iota((rows, width), 0) + first_row
            kept = factors[p, pl.ds(pl.multiple_of(first_row, 8), rows), :]
            out[...] = jnp.where(row >= iota((rows, width), 1), kept, out[...])


def update(shape, pieces, turned, place, rows, cols, factors, tiles, tile_place):
    count = place.shape[1]
    _, block_rows, depth = rows[0].shape
    whole = functools.partial(
        pl.BlockSpec, index_map=lambda n, at, tile: (0, 0, 0), pipeline_mode=pl.Buffered(1)
    )

    def held(array, index):
        return pl.BlockSpec((1,) + array.shape[1:], lambda n, at, tile: (at[index, n], 0, 0))

    specs = [held(array, 10 + len(rows) + i) for i, array in enumerate(pieces)]
    specs += [held(array, 10 + i) for i, array in enumerate(rows)]
    specs += [whole(array.shape) for array in (*cols, factors, tiles)]
    operands = [*pieces, *rows, *cols, factors, tiles]
    return pl.pallas_call(
        functools.partial(update_kernel, turned, len(rows)),
        grid_spec=pltpu.PrefetchScalarGridSpec(
            num_scalar_prefetch=2,
            grid=(count,),
            in_specs=specs,
            out_specs=pl.BlockSpec((block_rows, PANEL), lambda n, at, tile: (at[0, n], at[1, n])),
            scratch_shapes=[pltpu.VMEM((block_rows, depth), jnp.bfloat16)] * 2,
        ),
        out_shape=jax.ShapeDtypeStruct(shape, jnp.float32),
        compiler_params=pltpu.CompilerParams(vmem_limit_bytes=VMEM_LIMIT),
        cost_estimate=pl.CostEstimate(
            flops=6 * count * block_rows * PANEL * depth,
            bytes_accessed=count * block_rows * PANEL * 8,
            transcendentals=0,
        ),
        name="update",
    )(place.astype(jnp.int32), tile_place.astype(jnp.int32), *operands)


def add_kernel(turned, place, piece, before, out):
    step = pl.program_id(0)
    rows, width = out.shape
    first_row = place[5, step]
    panel = place[6, step]
    out[...] = before[...] + (piece[0].T if turned else piece[0])

    @pl.when((panel >= 0) & (first_row >= 0))
    def _():
        row = iota((rows, width), 0) + first_row
        out[...] = jnp.where(row >= iota((rows, width), 1), before[...], out[...])


def add_entries(front, pieces, place, turned):
    count = place.shape[1]
    rows, width = pieces.shape[1:]
    spot = pl.BlockSpec((rows, width), lambda n, at: (at[0, n], at[1, n]))
    return pl.pallas_call(
        functools.partial(add_kernel, turned),
        grid_spec=pltpu.PrefetchScalarGridSpec(
            num_scalar_prefetch=1,
            grid=(count,),
            in_specs=[pl.BlockSpec((1, rows, width), lambda n, at: (at[at.shape[0] - 1, n], 0, 0)), spot],
            out_specs=spot,
        ),
        out_shape=jax.ShapeDtypeStruct(front.shape, jnp.float32),
        input_output_aliases={2: 0},
        cost_estimate=pl.CostEstimate(
            flops=0, bytes_accessed=12 * count * rows * width, transcendentals=0
        ),
        name="add_entries",
    )(place.astype(jnp.int32), pieces, front)


def body(initial, child_tiles, child_targets):
    wide_size = lax.axis_size("wide")
    tall_size = lax.axis_size("tall")
    wide_at = lax.axis_index("wide")
    tall_at = lax.axis_index("tall")
    slab_rows, front_order = initial.shape
    tile_count, tile_edge, _ = child_tiles.shape
    per_row = tile_count // tall_size
    col_tiles = front_order // (PANEL * wide_size)
    blocks_per_panel = PANEL // slab_rows
    depth = PANELS * PANEL
    mirrored = wide_size == 8 and tall_size == 4 and slab_rows == PANEL and col_tiles == 4
    half = wide_at // 4
    level = wide_at // 2
    own_group = wide_at * tall_size + tall_at

    def number(w, t):
        return w * tall_size + t

    def everyone(target):
        return [
            (number(w, t), number(*target(w, t))) for w in range(wide_size) for t in range(tall_size)
        ]

    def grid(*sizes):
        axes = jnp.meshgrid(*[jnp.arange(n, dtype=jnp.int32) for n in sizes], indexing="ij")
        return [axis.reshape(-1) for axis in axes]

    j4 = jnp.arange(4, dtype=jnp.int32)
    if mirrored:
        near_d, near_a = grid(4, 2)
        near_columns = (2 * (1 - half) + near_a) * 8 + 4 * half + (near_d ^ wide_at % 4)
        near_sent = pack(initial, near_columns[4:])
        child_tiles, near_sent = lax.optimization_barrier((child_tiles, near_sent))
        near_got = lax.ppermute(near_sent, BOTH, everyone(lambda w, t: (w ^ 2, t)))
        near_own = pack(initial, near_columns[:4])

    target_rows = jnp.pad(
        child_targets.astype(jnp.float32)[:, None, :], ((0, 0), (0, 7), (0, tile_edge - 2))
    )
    marked = jnp.concatenate([child_tiles, target_rows], 1)
    row_tiles = lax.all_to_all(
        marked.reshape(tall_size, per_row, tile_edge + 8, tile_edge), "tall", 0, 0, tiled=True
    ).reshape(tile_count, tile_edge + 8, tile_edge)
    targets = row_tiles[:, tile_edge, :2].astype(jnp.int32)
    strip_cols = depth // tile_edge
    strip_index = (targets[:, 0] * tile_edge % slab_rows) // tile_edge * strip_cols + targets[:, 1]
    strip_index = jnp.where(targets[:, 1] < strip_cols, strip_index, -1)
    strip = add_blocks(
        initial[:, :depth],
        row_tiles[:, :tile_edge].reshape(tile_count, tile_edge * tile_edge),
        strip_index,
        tile_edge,
    )

    owner = (targets[:, 1] * tile_edge // PANEL % wide_size).reshape(tall_size, per_row)
    match = owner[None, :, :] == jnp.arange(wide_size, dtype=jnp.int32)[:, None, None]
    filled = jnp.any(match, axis=2).reshape(-1)
    chosen = jnp.argmax(match, axis=2).astype(jnp.int32)
    chosen = (chosen + jnp.arange(tall_size, dtype=jnp.int32)[None, :] * per_row).reshape(-1)
    slots = wide_size * tall_size
    outgoing = jnp.where(filled[:, None, None], jnp.take(row_tiles, chosen, axis=0), -1.0)
    tiles = lax.all_to_all(
        outgoing.reshape(wide_size, tall_size, tile_edge + 8, tile_edge), "wide", 0, 0, tiled=True
    ).reshape(slots, tile_edge + 8, tile_edge)

    block_rows = jnp.arange(wide_size, dtype=jnp.int32)
    block_cols = jnp.arange(col_tiles, dtype=jnp.int32)
    if mirrored:
        native = lax.all_gather(
            strip, "wide", axis=0, axis_index_groups=[[0, 2, 4, 6], [1, 3, 5, 7]]
        )
        core = wide_at % 2
        turned = []
        for e in range(4):
            pairs = []
            for z in range(4):
                for t in range(4):
                    pairs.append((number(2 * z + z // 2, t), number(2 * z + t % 2, t ^ e)))
            pairs = [pair for pair in pairs if pair[0] != pair[1]]
            packed = pack(initial, (4 * (1 - half) + j4) * tall_size + (tall_at ^ e))
            arrived = lax.ppermute(packed, BOTH, pairs)
            turned.append(arrived if e else jnp.where(core == half, packed, arrived))

        def from_tall(t):
            e = tall_at ^ t
            return jnp.where(
                e == 0, turned[0], jnp.where(e == 1, turned[1], jnp.where(e == 2, turned[2], turned[3]))
            )

        native, near_got, tiles, turned = lax.optimization_barrier((native, near_got, tiles, turned))

        dest, a = grid(8, 2)
        packed = pack(initial, (2 * half + a) * 8 + dest).reshape(8, 2, slab_rows, PANEL)
        packed, native = lax.optimization_barrier((packed, native))
        main = lax.all_to_all(packed, "wide", 0, 0, tiled=True).reshape(16, slab_rows, PANEL)

        evens = range(0, wide_size, 2)
        have = native[0]
        parts = [
            lax.ppermute(have, BOTH, [(number(w, t), number(w, t ^ e)) for w in evens for t in (0, 1)])
            for e in (1, 2, 3)
        ]
        top = jnp.where(
            tall_at == 0, have, jnp.where(tall_at == 1, parts[0], jnp.where(tall_at == 2, parts[1], parts[2]))
        )
        bottom = jnp.where(
            tall_at == 1, have, jnp.where(tall_at == 0, parts[0], jnp.where(tall_at == 3, parts[1], parts[2]))
        )
        square = jnp.concatenate([top, bottom], 0)
        other = lax.ppermute(
            square, BOTH, [(number(w, t), number(w + 1, t)) for w in evens for t in range(tall_size)]
        )
        diag = jnp.where(wide_at % 2 == 0, square, other)

        after, square, near_got, turned = lax.optimization_barrier((native, square, near_got, turned))
        near_mate = lax.ppermute(
            jnp.concatenate([near_own[2:], near_got[2:]], 0), BOTH, everyone(lambda w, t: (w ^ 1, t))
        )
        near = jnp.concatenate([near_own[:2], near_mate[:2], near_got[:2], near_mate[2:]], 0)
        moves = from_tall((1 - level % 2) * 2 + core)
        moved = lax.ppermute(moves, BOTH, everyone(lambda w, t: (w ^ 2, t)))
        stays = from_tall(level % 2 * 2 + core)
        column_raw = [native]
        for e in range(4):
            pairs = []
            for z in range(4):
                for x in range(2):
                    t = z % 2 * 2 + x
                    pairs.append((number(2 * z + z // 2, t), number(2 * z + x, t ^ e)))
            pairs = [pair for pair in pairs if pair[0] != pair[1]]
            column_raw.append(lax.ppermute(after if e > 1 else native, BOTH, pairs))
        column_from = tall_at ^ (level % 2 * 2 + core)
        column_from = jnp.where((column_from == 0) & (core == half), 0, 1 + column_from)
    else:
        gathered = lax.all_gather(strip, "tall", axis=0, tiled=True)[:depth]
        diag = lax.psum(jnp.where(wide_at == 0, gathered, 0.0), "wide")

    marks = tiles[:, tile_edge, :2].astype(jnp.int32)
    at_row = marks[:, 0] * tile_edge
    at_col = marks[:, 1] * tile_edge
    block_number = at_row // slab_rows // tall_size * col_tiles + at_col // PANEL // wide_size
    block_number = jnp.where(marks[:, 0] >= 0, block_number, -1)
    lane = jnp.arange(slots, dtype=jnp.int32)
    ahead = block_number[None, :] < block_number[:, None]
    ahead |= (block_number[None, :] == block_number[:, None]) & (lane[None, :] < lane[:, None])
    rank = jnp.sum(ahead.astype(jnp.int32), axis=1)
    order = jnp.sum(jnp.where(rank[:, None] == lane[None, :], lane[:, None], 0), axis=0)
    tile_place = jnp.stack(
        [
            order,
            jnp.take(at_row % slab_rows // tile_edge, order),
            jnp.take(at_col % PANEL // tile_edge, order),
        ]
    )

    factors, inverses, below = factor_panels(diag)
    if mirrored:
        native_rows = 2 * j4 + core
        (native,) = solve([native], 0, (native_rows * tall_size + tall_at) * slab_rows, inverses, below)
        across = lax.ppermute(native, BOTH, everyone(lambda w, t: (w ^ 1, t)))
        first = (block_cols * wide_size + wide_at) * PANEL
        cols = solve(column_raw, column_from, first, inverses, below, True)
        rows = [native, across]
    else:
        (own,) = solve([strip[None]], 0, own_group[None] * slab_rows, inverses, below)
        solved = lax.all_gather(own[0], "wide", axis=0)
        wanted = (
            (np.arange(col_tiles)[None, :, None] * wide_size + np.arange(wide_size)[:, None, None])
            * blocks_per_panel
            + np.arange(blocks_per_panel)[None, None, :]
        ).reshape(wide_size, col_tiles * blocks_per_panel)
        senders, receivers = block_tables(wanted, tall_size)
        piece = jnp.take(solved, jnp.asarray(senders)[wide_at, tall_at], axis=0)
        pieces = lax.all_gather(piece, "tall", axis=0, tiled=True)
        column_rows = jnp.take(pieces, jnp.asarray(receivers)[wide_at], axis=0)
        column_rows = column_rows.reshape(col_tiles, PANEL, depth).transpose(0, 2, 1)
        high = lax.reduce_precision(column_rows, 8, 7)
        cols = [high.astype(jnp.bfloat16), (column_rows - high).astype(jnp.bfloat16)]
        rows = [solved]

    def places(block_row, block_col, row_slot, kind, piece_slots):
        first = (block_row * tall_size + tall_at) * slab_rows
        panel = block_col * wide_size + wide_at
        panel = jnp.where(panel < PANELS, panel, -1)
        per = rows[0].shape[0]
        table = [
            block_row,
            block_col,
            jnp.sum(block_number[None, :] < (block_row * col_tiles + block_col)[:, None], axis=1),
            row_slot,
            block_col,
            first - panel * PANEL,
            panel,
            kind,
            row_slot // per,
            jnp.sum(block_number[None, :] <= (block_row * col_tiles + block_col)[:, None], axis=1),
        ]
        table += [jnp.clip(row_slot - per * i, 0, per - 1) for i in range(len(rows))]
        return jnp.stack([jnp.asarray(line, jnp.int32) for line in table + piece_slots])

    shape = (wide_size * slab_rows, col_tiles * PANEL)
    rest = (rows, cols, factors, tiles, tile_place)
    if not mirrored:
        dest, q = grid(wide_size, col_tiles)
        packed = pack(initial, q * wide_size + dest).reshape(wide_size, col_tiles, slab_rows, PANEL)
        arrived = lax.all_to_all(packed, "wide", 0, 0, tiled=True)
        arrived = arrived.reshape(wide_size * col_tiles, slab_rows, PANEL)
        place = places(dest, q, dest, jnp.zeros_like(dest), [dest * col_tiles + q])
        return update(shape, [arrived], (False,), place, *rest)

    slot, q = grid(8, 4)
    k = 2 * (slot % 4) + jnp.where(slot < 4, core, 1 - core)
    d = wide_at ^ k
    same = d < 4
    kind = jnp.where(same & (q // 2 != half), 0, jnp.where(~same & (q == level), 1, 2))
    near_slot = jnp.where(same, d * 2 + q % 2, 3)
    stays_slot = jnp.where(same, 0, k % 4)
    place = places(k, q, slot, kind, [near_slot, stays_slot])
    front = update(shape, [near, stays], (False, True), place, *rest)
    k = 4 * (1 - half) + j4
    place = places(k, jnp.zeros_like(k) + (level ^ 1), k, k, [j4])
    front = add_entries(front, moved, place, True)
    k, a = grid(8, 2)
    place = places(k, 2 * (k // 4) + a, k, k, [2 * k + a])
    return add_entries(front, main, place, False)


def solution(mesh):
    return jax.shard_map(
        body,
        mesh=mesh,
        in_specs=(
            P(("wide", "tall"), None),
            P(("wide", "tall"), None, None),
            P(("wide", "tall"), None),
        ),
        out_specs=P("tall", "wide"),
        check_vma=False,
    )
```

```python
import functools

import jax
import jax.numpy as jnp
import numpy as np
from jax import lax
from jax.experimental import pallas as pl
from jax.experimental.pallas import tpu as pltpu
from jax.sharding import PartitionSpec as P

PANEL = 512
PANELS = 2
BOTH = ("wide", "tall")
VMEM_LIMIT = 56 * 1024 * 1024
full_precision = lax.Precision.HIGHEST


def full_dot(left, right, dims=((1,), (0,))):
    return lax.dot_general(
        left, right, (dims, ((), ())), precision=full_precision, preferred_element_type=jnp.float32
    )


def iota(shape, axis):
    return lax.broadcasted_iota(jnp.int32, shape, axis)


def factor_block(work, edge):
    group = 8
    wide = 2 * edge
    lanes = iota((group, edge), 1)
    row = iota((group, 1), 0)

    def step(s, carry):
        low = pl.multiple_of(s * group, group)
        strip = work[pl.ds(low, group), :]
        left = strip[:, :edge]
        cols = [
            jnp.sum(jnp.where(lanes == low + i, left, 0.0), axis=1, keepdims=True)
            for i in range(group)
        ]
        for i in range(group):
            pivot = cols[i][i : i + 1]
            scale = lax.rsqrt(pivot)
            scale = scale * (1.5 - 0.5 * pivot * scale * scale)
            column = jnp.where(row > i, cols[i] * scale, 0.0)
            top = strip[i : i + 1] * scale
            strip = jnp.where(row == i, top, strip - column * top)
            for m in range(i + 1, group):
                cols[m] = cols[m] - column * column[m : m + 1]
        work[pl.ds(low, group), :] = strip
        left = jnp.where(lanes >= low + group, strip[:, :edge], 0.0)
        work[...] = work[...] - full_dot(left, strip, ((0,), (0,)))
        return carry

    lax.fori_loop(0, edge // group, step, 0)


def factor_kernel(diag, factors, inverses, below, square, work):
    edge = work.shape[0]
    wide = PANEL
    lower = iota((wide, wide), 0) >= iota((wide, wide), 1)
    small = iota((edge, edge), 0) >= iota((edge, edge), 1)
    eye = (iota((edge, edge), 0) == iota((edge, edge), 1)).astype(jnp.float32)
    steps = wide // edge
    for p in range(PANELS):
        own = pl.ds(p * wide, wide)
        block = diag[own, own]
        block = jnp.where(lower, block, block.T)
        for before in range(p):
            rows = below[pl.ds((p - 1) * wide, wide), pl.ds(before * wide, wide)]
            block = block - full_dot(rows, rows, ((1,), (1,)))
        square[...] = block
        factors[p] = jnp.zeros((wide, wide), jnp.float32)
        inverses[p] = jnp.zeros((wide, wide), jnp.float32)
        for b in range(steps):
            at = pl.ds(b * edge, edge)
            work[:, :edge] = square[at, at]
            work[:, edge:] = eye
            factor_block(work, edge)
            factors[p, at, at] = jnp.where(small, work[:, :edge].T, 0.0)
            inverse = jnp.where(small, work[:, edge:], 0.0)
            inverses[p, at, at] = inverse
            if b + 1 < steps:
                rest = pl.ds((b + 1) * edge, wide - (b + 1) * edge)
                under = full_dot(square[rest, at], inverse, ((1,), (1,)))
                factors[p, rest, at] = under
                square[rest, rest] = square[rest, rest] - full_dot(under, under, ((1,), (1,)))
            if b > 0:
                past = pl.ds(0, b * edge)
                inner = full_dot(factors[p, at, past], inverses[p, past, past])
                inverses[p, at, past] = -full_dot(inverse, inner)
        for after in range(p + 1, PANELS):
            there = pl.ds(after * wide, wide)
            rows = diag[there, own]
            for before in range(p):
                rows = rows - full_dot(
                    below[pl.ds((after - 1) * wide, wide), pl.ds(before * wide, wide)],
                    below[pl.ds((p - 1) * wide, wide), pl.ds(before * wide, wide)],
                    ((1,), (1,)),
                )
            below[pl.ds((after - 1) * wide, wide), own] = full_dot(rows, inverses[p], ((1,), (1,)))


def add_blocks(base, tiles, block_index, tile_edge):
    base_rows, base_cols = base.shape
    row_count = base_rows // tile_edge
    col_count = base_cols // tile_edge
    slot_ids = jnp.arange(row_count * col_count, dtype=jnp.int32)
    selector = (slot_ids[:, None] == block_index[None, :]).astype(jnp.float32)
    summed = full_dot(selector, tiles)
    summed = summed.reshape(row_count, col_count, tile_edge, tile_edge).transpose(0, 2, 1, 3)
    return base + summed.reshape(base_rows, base_cols)


def block_tables(wanted, tall_size):
    owners = wanted % tall_size
    slots_at = wanted // tall_size
    width_wanted = wanted.shape[1]
    same_owner = owners[:, :, None] == owners[:, None, :]
    earlier = np.tril(np.ones((width_wanted, width_wanted), dtype=np.int32), -1)[None, :, :] > 0
    ranks = np.sum(same_owner & earlier, axis=2)
    piece_depth = int(np.max(ranks)) + 1
    talls = np.arange(tall_size)
    places = np.arange(piece_depth)
    matches = (owners[:, None, None, :] == talls[None, :, None, None]) & (
        ranks[:, None, None, :] == places[None, None, :, None]
    )
    senders = np.sum(matches * slots_at[:, None, None, :], axis=3).astype(np.int32)
    receivers = (owners * piece_depth + ranks).astype(np.int32)
    return (senders, receivers)


def copy_kernel(table, source, target):
    target[0] = source[...]


def pack(slab, columns):
    rows = slab.shape[0]
    count = columns.shape[0]
    return pl.pallas_call(
        copy_kernel,
        grid_spec=pltpu.PrefetchScalarGridSpec(
            num_scalar_prefetch=1,
            grid=(count,),
            in_specs=[pl.BlockSpec((rows, PANEL), lambda n, table: (0, table[n]))],
            out_specs=pl.BlockSpec((1, rows, PANEL), lambda n, table: (n, 0, 0)),
        ),
        out_shape=jax.ShapeDtypeStruct((count, rows, PANEL), jnp.float32),
        cost_estimate=pl.CostEstimate(
            flops=0, bytes_accessed=2 * count * rows * PANEL * 4, transcendentals=0
        ),
        name="pack",
    )(columns.astype(jnp.int32), slab)


def factor_panels(diag):
    square = jax.ShapeDtypeStruct((PANELS, PANEL, PANEL), jnp.float32)
    rest = (PANELS - 1) * PANEL
    edge = 128
    return pl.pallas_call(
        factor_kernel,
        out_shape=(square, square, jax.ShapeDtypeStruct((rest, rest), jnp.float32)),
        scratch_shapes=[
            pltpu.VMEM((PANEL, PANEL), jnp.float32),
            pltpu.VMEM((edge, 2 * edge), jnp.float32),
        ],
        compiler_params=pltpu.CompilerParams(vmem_limit_bytes=VMEM_LIMIT),
        cost_estimate=pl.CostEstimate(
            flops=1_000_000_000, bytes_accessed=1_000_000, transcendentals=0
        ),
        name="factor",
    )(diag)


def split(value):
    high = value.astype(jnp.bfloat16)
    return high, (value - high.astype(jnp.float32)).astype(jnp.bfloat16)


def solve_kernel(turned, parts, table, *refs):
    inverses, below = refs[2 * parts : 2 * parts + 2]
    outs, raw = refs[2 * parts + 2 : -1], refs[-1]
    rows = raw.shape[0]
    for i in range(parts):

        @pl.when(table[1, 0] == i)
        def _(i=i):
            raw[:, :PANEL] = refs[i][0]
            raw[:, PANEL:] = refs[parts + i][0]

    at = table[0, pl.program_id(0)] + iota((rows, 1), 0)
    solved_0 = full_dot(raw[:, :PANEL], inverses[0], ((1,), (1,)))
    solved_0 = jnp.where(at >= PANEL, solved_0, 0.0)
    right = raw[:, PANEL:] - full_dot(solved_0, below[...], ((1,), (1,)))
    solved_1 = full_dot(right, inverses[1], ((1,), (1,)))
    solved_1 = jnp.where(at >= 2 * PANEL, solved_1, 0.0)
    for p, part in enumerate((solved_0, solved_1)):
        span = pl.ds(p * PANEL, PANEL)
        if turned:
            outs[0][0, span, :], outs[1][0, span, :] = split(part.T)
        else:
            outs[0][0, :, span] = part


def solve(raws_0, raws_1, which, first_row, inverses, below, turned=False):
    count, rows, width = raws_0[0].shape
    depth = PANELS * width
    parts = len(raws_0)
    if turned:
        out_shape = [jax.ShapeDtypeStruct((count, depth, rows), jnp.bfloat16)] * 2
        out_specs = [pl.BlockSpec((1, depth, rows), lambda n, table: (n, 0, 0))] * 2
    else:
        out_shape = [jax.ShapeDtypeStruct((count, rows, depth), jnp.float32)]
        out_specs = [pl.BlockSpec((1, rows, depth), lambda n, table: (n, 0, 0))]

    def held(i):
        return pl.BlockSpec(
            (1, rows, width), lambda n, table: (jnp.where(table[1, 0] == i, n, 0), 0, 0)
        )

    table = jnp.stack([first_row, jnp.full_like(first_row, 1) * which]).astype(jnp.int32)
    return pl.pallas_call(
        functools.partial(solve_kernel, turned, parts),
        grid_spec=pltpu.PrefetchScalarGridSpec(
            num_scalar_prefetch=1,
            grid=(count,),
            in_specs=[held(i) for i in [*range(parts), *range(parts)]]
            + [
                pl.BlockSpec(inverses.shape, lambda n, table: (0, 0, 0)),
                pl.BlockSpec(below.shape, lambda n, table: (0, 0)),
            ],
            out_specs=out_specs,
            scratch_shapes=[pltpu.VMEM((rows, depth), jnp.float32)],
        ),
        out_shape=out_shape,
        compiler_params=pltpu.CompilerParams(vmem_limit_bytes=VMEM_LIMIT),
        cost_estimate=pl.CostEstimate(
            flops=count * rows * PANEL * PANEL, bytes_accessed=count * rows * depth,
            transcendentals=0,
        ),
        name="solve",
    )(table, *raws_0, *raws_1, inverses, below)


def update_kernel(turned, row_parts, place, tile_place, *refs):
    pieces = refs[: len(turned)]
    row_refs = refs[len(turned) : len(turned) + row_parts]
    col_hi, col_lo, factors, tiles = refs[len(turned) + row_parts : len(turned) + row_parts + 4]
    out, row_hi, row_lo = refs[-3:]
    step = pl.program_id(0)
    rows, width = out.shape
    edge = tiles.shape[2]
    slot = place[3, step]
    at = place[4, step]
    first_row = place[5, step]
    panel = place[6, step]
    kind = place[7, step]
    fresh = (step == 0) | (slot != place[3, jnp.maximum(step - 1, 0)])
    for i, ref in enumerate(row_refs):

        @pl.when(fresh & (place[8, step] == i))
        def _(ref=ref):
            row_hi[...], row_lo[...] = split(ref[0])

    for i, ref in enumerate(pieces):

        @pl.when(kind == i)
        def _(i=i, ref=ref):
            out[...] = ref[0].T if turned[i] else ref[0]

    change = jnp.dot(row_hi[...], col_hi[at], preferred_element_type=jnp.float32)
    change += jnp.dot(row_hi[...], col_lo[at], preferred_element_type=jnp.float32)
    change += jnp.dot(row_lo[...], col_hi[at], preferred_element_type=jnp.float32)

    @pl.when(kind >= len(pieces))
    def _():
        out[...] = -change

    @pl.when(kind < len(pieces))
    def _():
        out[...] = out[...] - change

    def add_tile(n, carry):
        at_row = pl.multiple_of(tile_place[1, n] * edge, edge)
        at_col = pl.multiple_of(tile_place[2, n] * edge, edge)
        spot = (pl.ds(at_row, edge), pl.ds(at_col, edge))
        out[spot] = out[spot] + tiles[tile_place[0, n], :edge, :]
        return carry

    lax.fori_loop(place[2, step], place[9, step], add_tile, 0)
    for p in range(PANELS):
        for i, ref in enumerate(row_refs):

            @pl.when((panel == p) & (first_row >= width) & (place[8, step] == i))
            def _(p=p, ref=ref):
                out[...] = ref[0, :, p * PANEL : (p + 1) * PANEL]

        @pl.when((panel == p) & (first_row >= 0) & (first_row < width))
        def _(p=p):
            row = iota((rows, width), 0) + first_row
            kept = factors[p, pl.ds(pl.multiple_of(first_row, 8), rows), :]
            out[...] = jnp.where(row >= iota((rows, width), 1), kept, out[...])


def update(shape, pieces, turned, place, rows, cols, factors, tiles, tile_place):
    count = place.shape[1]
    _, block_rows, depth = rows[0].shape
    whole = functools.partial(
        pl.BlockSpec, index_map=lambda n, at, tile: (0, 0, 0), pipeline_mode=pl.Buffered(1)
    )

    def held(array, index):
        return pl.BlockSpec((1,) + array.shape[1:], lambda n, at, tile: (at[index, n], 0, 0))

    specs = [held(array, 10 + len(rows) + i) for i, array in enumerate(pieces)]
    specs += [held(array, 10 + i) for i, array in enumerate(rows)]
    specs += [whole(array.shape) for array in (*cols, factors, tiles)]
    operands = [*pieces, *rows, *cols, factors, tiles]
    return pl.pallas_call(
        functools.partial(update_kernel, turned, len(rows)),
        grid_spec=pltpu.PrefetchScalarGridSpec(
            num_scalar_prefetch=2,
            grid=(count,),
            in_specs=specs,
            out_specs=pl.BlockSpec((block_rows, PANEL), lambda n, at, tile: (at[0, n], at[1, n])),
            scratch_shapes=[pltpu.VMEM((block_rows, depth), jnp.bfloat16)] * 2,
        ),
        out_shape=jax.ShapeDtypeStruct(shape, jnp.float32),
        compiler_params=pltpu.CompilerParams(vmem_limit_bytes=VMEM_LIMIT),
        cost_estimate=pl.CostEstimate(
            flops=count * block_rows * PANEL * PANEL, bytes_accessed=count * block_rows * PANEL,
            transcendentals=0,
        ),
        name="update",
    )(place.astype(jnp.int32), tile_place.astype(jnp.int32), *operands)


def add_kernel(turned, place, piece, before, out):
    step = pl.program_id(0)
    rows, width = out.shape
    first_row = place[5, step]
    panel = place[6, step]
    out[...] = before[...] + (piece[0].T if turned else piece[0])

    @pl.when((panel >= 0) & (first_row >= 0))
    def _():
        row = iota((rows, width), 0) + first_row
        out[...] = jnp.where(row >= iota((rows, width), 1), before[...], out[...])


def add_entries(front, pieces, place, turned):
    count = place.shape[1]
    rows, width = pieces.shape[1:]
    spot = pl.BlockSpec((rows, width), lambda n, at: (at[0, n], at[1, n]))
    return pl.pallas_call(
        functools.partial(add_kernel, turned),
        grid_spec=pltpu.PrefetchScalarGridSpec(
            num_scalar_prefetch=1,
            grid=(count,),
            in_specs=[pl.BlockSpec((1, rows, width), lambda n, at: (at[at.shape[0] - 1, n], 0, 0)), spot],
            out_specs=spot,
        ),
        out_shape=jax.ShapeDtypeStruct(front.shape, jnp.float32),
        input_output_aliases={2: 0},
        cost_estimate=pl.CostEstimate(
            flops=0, bytes_accessed=12 * count * rows * width, transcendentals=0
        ),
        name="add_entries",
    )(place.astype(jnp.int32), pieces, front)


def body(initial, child_tiles, child_targets):
    wide_size = lax.axis_size("wide")
    tall_size = lax.axis_size("tall")
    wide_at = lax.axis_index("wide")
    tall_at = lax.axis_index("tall")
    slab_rows, front_order = initial.shape
    tile_count, tile_edge, _ = child_tiles.shape
    per_row = tile_count // tall_size
    col_tiles = front_order // (PANEL * wide_size)
    blocks_per_panel = PANEL // slab_rows
    depth = PANELS * PANEL
    mirrored = wide_size == 8 and tall_size == 4 and slab_rows == PANEL and col_tiles == 4
    half = wide_at // 4
    level = wide_at // 2
    own_group = wide_at * tall_size + tall_at

    def number(w, t):
        return w * tall_size + t

    def everyone(target):
        return [
            (number(w, t), number(*target(w, t))) for w in range(wide_size) for t in range(tall_size)
        ]

    def grid(*sizes):
        axes = jnp.meshgrid(*[jnp.arange(n, dtype=jnp.int32) for n in sizes], indexing="ij")
        return [axis.reshape(-1) for axis in axes]

    j4 = jnp.arange(4, dtype=jnp.int32)
    if mirrored:
        near_d, near_a = grid(4, 2)
        near_columns = (2 * (1 - half) + near_a) * 8 + 4 * half + (near_d ^ wide_at % 4)
        near_sent = pack(initial, near_columns[4:])
        child_tiles, near_sent = lax.optimization_barrier((child_tiles, near_sent))
        near_got = lax.ppermute(near_sent, BOTH, everyone(lambda w, t: (w ^ 2, t)))
        near_own = pack(initial, near_columns[:4])

    target_rows = jnp.pad(
        child_targets.astype(jnp.float32)[:, None, :], ((0, 0), (0, 7), (0, tile_edge - 2))
    )
    marked = jnp.concatenate([child_tiles, target_rows], 1)
    row_tiles = lax.all_to_all(
        marked.reshape(tall_size, per_row, tile_edge + 8, tile_edge), "tall", 0, 0, tiled=True
    ).reshape(tile_count, tile_edge + 8, tile_edge)
    targets = row_tiles[:, tile_edge, :2].astype(jnp.int32)
    strip_cols = depth // tile_edge
    strip_index = (targets[:, 0] * tile_edge % slab_rows) // tile_edge * strip_cols + targets[:, 1]
    strip_index = jnp.where(targets[:, 1] < strip_cols, strip_index, -1)
    strip = add_blocks(
        initial[:, :depth],
        row_tiles[:, :tile_edge].reshape(tile_count, tile_edge * tile_edge),
        strip_index,
        tile_edge,
    )

    owner = (targets[:, 1] * tile_edge // PANEL % wide_size).reshape(tall_size, per_row)
    match = owner[None, :, :] == jnp.arange(wide_size, dtype=jnp.int32)[:, None, None]
    filled = jnp.any(match, axis=2).reshape(-1)
    chosen = jnp.argmax(match, axis=2).astype(jnp.int32)
    chosen = (chosen + jnp.arange(tall_size, dtype=jnp.int32)[None, :] * per_row).reshape(-1)
    slots = wide_size * tall_size
    outgoing = jnp.where(filled[:, None, None], jnp.take(row_tiles, chosen, axis=0), -1.0)
    if mirrored:
        turned_sent = [pack(initial, (4 * (1 - half) + j4) * tall_size + (tall_at ^ e)) for e in range(4)]
    tiles = lax.all_to_all(
        outgoing.reshape(wide_size, tall_size, tile_edge + 8, tile_edge), "wide", 0, 0, tiled=True
    ).reshape(slots, tile_edge + 8, tile_edge)

    block_rows = jnp.arange(wide_size, dtype=jnp.int32)
    block_cols = jnp.arange(col_tiles, dtype=jnp.int32)
    if mirrored:
        core = wide_at % 2
        turned = []
        for e in range(4):
            pairs = []
            for z in range(4):
                for t in range(4):
                    pairs.append((number(2 * z + z // 2, t), number(2 * z + t % 2, t ^ e)))
            pairs = [pair for pair in pairs if pair[0] != pair[1]]
            arrived = lax.ppermute(turned_sent[e], BOTH, pairs)
            turned.append(arrived if e else jnp.where(core == half, turned_sent[0], arrived))

        same_core = [[0, 2, 4, 6], [1, 3, 5, 7]]
        left, near_got, tiles, turned = lax.optimization_barrier(
            (strip[:, :PANEL], near_got, tiles, turned)
        )
        native_0 = lax.all_gather(left, "wide", axis=0, axis_index_groups=same_core)
        dest, a = grid(8, 2)
        packed = pack(initial, (2 * half + a) * 8 + dest).reshape(8, 2, slab_rows, PANEL)
        right, native_0, packed = lax.optimization_barrier((strip[:, PANEL:], native_0, packed))
        native_1 = lax.all_gather(right, "wide", axis=0, axis_index_groups=same_core)

        def to_columns(native):
            arrived = [native]
            for e in range(4):
                pairs = []
                for z in range(4):
                    for x in range(2):
                        t = z % 2 * 2 + x
                        pairs.append((number(2 * z + z // 2, t), number(2 * z + x, t ^ e)))
                pairs = [pair for pair in pairs if pair[0] != pair[1]]
                arrived.append(lax.ppermute(native, BOTH, pairs))
            return arrived

        columns_0 = to_columns(native_0)
        def from_tall(t):
            e = tall_at ^ t
            return jnp.where(
                e == 0, turned[0], jnp.where(e == 1, turned[1], jnp.where(e == 2, turned[2], turned[3]))
            )

        moves = from_tall((1 - level % 2) * 2 + core)
        stays = from_tall(level % 2 * 2 + core)
        near_mate = lax.ppermute(
            jnp.concatenate([near_own[2:], near_got[2:]], 0), BOTH, everyone(lambda w, t: (w ^ 1, t))
        )
        near = jnp.concatenate([near_own[:2], near_mate[:2], near_got[:2], near_mate[2:]], 0)
        native_1, near, moves, stays, columns_0 = lax.optimization_barrier(
            (native_1, near, moves, stays, columns_0)
        )

        main = lax.all_to_all(packed, "wide", 0, 0, tiled=True).reshape(16, slab_rows, PANEL)

        evens = range(0, wide_size, 2)
        have = jnp.concatenate([native_0[0], native_1[0]], 1)
        parts = [
            lax.ppermute(have, BOTH, [(number(w, t), number(w, t ^ e)) for w in evens for t in (0, 1)])
            for e in (1, 2, 3)
        ]
        top = jnp.where(
            tall_at == 0, have, jnp.where(tall_at == 1, parts[0], jnp.where(tall_at == 2, parts[1], parts[2]))
        )
        bottom = jnp.where(
            tall_at == 1, have, jnp.where(tall_at == 0, parts[0], jnp.where(tall_at == 3, parts[1], parts[2]))
        )
        square = jnp.concatenate([top, bottom], 0)
        other = lax.ppermute(
            square, BOTH, [(number(w, t), number(w + 1, t)) for w in evens for t in range(tall_size)]
        )
        diag = jnp.where(wide_at % 2 == 0, square, other)

        moved = lax.ppermute(moves, BOTH, everyone(lambda w, t: (w ^ 2, t)))
        columns_1 = to_columns(native_1)
        column_from = tall_at ^ (level % 2 * 2 + core)
        column_from = jnp.where((column_from == 0) & (core == half), 0, 1 + column_from)
    else:
        gathered = lax.all_gather(strip, "tall", axis=0, tiled=True)[:depth]
        diag = lax.psum(jnp.where(wide_at == 0, gathered, 0.0), "wide")

    marks = tiles[:, tile_edge, :2].astype(jnp.int32)
    at_row = marks[:, 0] * tile_edge
    at_col = marks[:, 1] * tile_edge
    block_number = at_row // slab_rows // tall_size * col_tiles + at_col // PANEL // wide_size
    block_number = jnp.where(marks[:, 0] >= 0, block_number, -1)
    lane = jnp.arange(slots, dtype=jnp.int32)
    ahead = block_number[None, :] < block_number[:, None]
    ahead |= (block_number[None, :] == block_number[:, None]) & (lane[None, :] < lane[:, None])
    rank = jnp.sum(ahead.astype(jnp.int32), axis=1)
    order = jnp.sum(jnp.where(rank[:, None] == lane[None, :], lane[:, None], 0), axis=0)
    tile_place = jnp.stack(
        [
            order,
            jnp.take(at_row % slab_rows // tile_edge, order),
            jnp.take(at_col % PANEL // tile_edge, order),
        ]
    )

    factors, inverses, below = factor_panels(diag)
    if mirrored:
        factors, inverses, below, columns_1 = lax.optimization_barrier((factors, inverses, below, columns_1))
        native_rows = 2 * j4 + core
        (native,) = solve([native_0], [native_1], 0, (native_rows * tall_size + tall_at) * slab_rows, inverses, below)
        across = lax.ppermute(native, BOTH, everyone(lambda w, t: (w ^ 1, t)))
        first = (block_cols * wide_size + wide_at) * PANEL
        cols = solve(columns_0, columns_1, column_from, first, inverses, below, True)
        rows = [native, across]
    else:
        (own,) = solve(
            [strip[None, :, :PANEL]], [strip[None, :, PANEL:]], 0, own_group[None] * slab_rows, inverses, below
        )
        solved = lax.all_gather(own[0], "wide", axis=0)
        wanted = (
            (np.arange(col_tiles)[None, :, None] * wide_size + np.arange(wide_size)[:, None, None])
            * blocks_per_panel
            + np.arange(blocks_per_panel)[None, None, :]
        ).reshape(wide_size, col_tiles * blocks_per_panel)
        senders, receivers = block_tables(wanted, tall_size)
        piece = jnp.take(solved, jnp.asarray(senders)[wide_at, tall_at], axis=0)
        pieces = lax.all_gather(piece, "tall", axis=0, tiled=True)
        column_rows = jnp.take(pieces, jnp.asarray(receivers)[wide_at], axis=0)
        column_rows = column_rows.reshape(col_tiles, PANEL, depth).transpose(0, 2, 1)
        high = lax.reduce_precision(column_rows, 8, 7)
        cols = [high.astype(jnp.bfloat16), (column_rows - high).astype(jnp.bfloat16)]
        rows = [solved]

    def places(block_row, block_col, row_slot, kind, piece_slots):
        first = (block_row * tall_size + tall_at) * slab_rows
        panel = block_col * wide_size + wide_at
        panel = jnp.where(panel < PANELS, panel, -1)
        per = rows[0].shape[0]
        table = [
            block_row,
            block_col,
            jnp.sum(block_number[None, :] < (block_row * col_tiles + block_col)[:, None], axis=1),
            row_slot,
            block_col,
            first - panel * PANEL,
            panel,
            kind,
            row_slot // per,
            jnp.sum(block_number[None, :] <= (block_row * col_tiles + block_col)[:, None], axis=1),
        ]
        table += [jnp.clip(row_slot - per * i, 0, per - 1) for i in range(len(rows))]
        return jnp.stack([jnp.asarray(line, jnp.int32) for line in table + piece_slots])

    shape = (wide_size * slab_rows, col_tiles * PANEL)
    rest = (rows, cols, factors, tiles, tile_place)
    if not mirrored:
        dest, q = grid(wide_size, col_tiles)
        packed = pack(initial, q * wide_size + dest).reshape(wide_size, col_tiles, slab_rows, PANEL)
        arrived = lax.all_to_all(packed, "wide", 0, 0, tiled=True)
        arrived = arrived.reshape(wide_size * col_tiles, slab_rows, PANEL)
        place = places(dest, q, dest, jnp.zeros_like(dest), [dest * col_tiles + q])
        return update(shape, [arrived], (False,), place, *rest)

    slot, q = grid(8, 4)
    k = 2 * (slot % 4) + jnp.where(slot < 4, core, 1 - core)
    d = wide_at ^ k
    same = d < 4
    kind = jnp.where(same & (q // 2 != half), 0, jnp.where(~same & (q == level), 1, 2))
    near_slot = jnp.where(same, d * 2 + q % 2, 3)
    stays_slot = jnp.where(same, 0, k % 4)
    place = places(k, q, slot, kind, [near_slot, stays_slot])
    front = update(shape, [near, stays], (False, True), place, *rest)
    k = 4 * (1 - half) + j4
    place = places(k, jnp.zeros_like(k) + (level ^ 1), k, k, [j4])
    front = add_entries(front, moved, place, True)
    k, a = grid(8, 2)
    place = places(k, 2 * (k // 4) + a, k, k, [2 * k + a])
    return add_entries(front, main, place, False)


def solution(mesh):
    return jax.shard_map(
        body,
        mesh=mesh,
        in_specs=(
            P(("wide", "tall"), None),
            P(("wide", "tall"), None, None),
            P(("wide", "tall"), None),
        ),
        out_specs=P("tall", "wide"),
        check_vma=False,
    )
```
